32 devices in a mesh: row: 2 (over x), col: 4 (over z), rep: 4 (over y, core).
Axes of the slice: x: 2, y: 2, z: 4, core: 2. Of those that a mesh axis runs over, the one named last changes fastest.
Arguments:
- features: float32 [16384, 256], P(('row', 'col', 'rep')), may hold values from -6 to 6
- self_weight: float32 [256, 256], replicated, may hold values from -0.375 to 0.375
- neigh_weight: float32 [256, 256], replicated, may hold values from -1.2 to 1.2
- block_source: int32 [256, 8], P(('row', 'col', 'rep')), may hold values from 0 to 95, as said below
- edge_weights: int32 [256, 8, 64, 64], P(('row', 'col', 'rep')), may hold values from 0 to 15, as said below
- labels: int32 [16384], P(('row', 'col', 'rep')), may hold values from 0 to 255
Outputs:
- grad_self: float32 [256, 256], replicated
- grad_neigh: float32 [256, 256], replicated
- grad_features: float32 [16384, 256], P(('row', 'col', 'rep'))
The draws below stay inside these ranges and needn't reach their ends.
Inputs may be any that keep to these rules, and one draw needn't show every extreme that they name: `block_source`: slot 0 of every block row names the row's own block. `edge_weights`: in each block row the filled slots come first, with entries 1 to 15; later slots are all zero. Every block row has 1 to 8 filled slots, and some block row has all 8.
All inputs are finite; a program needn't handle non-finite values.
Results may differ from the reference program's by a relative error of at most 0.0035.
Values may be sent and summed in bfloat16 or wider, within the bound.
No kernel may reach another device: no remote copies, remote signals or barrier semaphores. Data moves between devices by JAX's collectives and lax.ppermute only.
A program may use at most 64 MiB of HBM per device.

```python
import jax
import jax.numpy as jnp
from jax import lax

FEAT = 256
CLASSES = 256
BLOCK = 64
SLOTS = 8
ROWS_DEV = 512
GROUP = 2048
NODES = 16384
BLOCKS = 256
N_COL = 4
N_REP = 4


def slot_counts(key):
    block_count = ROWS_DEV // BLOCK
    device_total = NODES // ROWS_DEV
    first_key, second_key, third_key, fourth_key = jax.random.split(jax.random.fold_in(key, 11), 4)
    level = jax.random.randint(first_key, (device_total,), 2, SLOTS + 1)
    chosen = jax.random.randint(second_key, (), 0, device_total)
    level = jnp.where(jnp.arange(device_total) == chosen, SLOTS, level)
    per_block = jnp.repeat(level, block_count)
    lowest = jnp.maximum(per_block - 3, 1)
    counts = jax.random.randint(third_key, (BLOCKS,), lowest, per_block + 1)
    target_spot = chosen * block_count + jax.random.randint(fourth_key, (), 0, block_count)
    return jnp.where(jnp.arange(BLOCKS) == target_spot, SLOTS, counts)


def draw_edge_weights(key, part):
    counts = slot_counts(key)
    values = jax.random.randint(jax.random.fold_in(key, 23), (BLOCKS, SLOTS, BLOCK, BLOCK), 1, 16)
    filled = jnp.arange(SLOTS)[None, :] < counts[:, None]
    return jnp.where(filled[:, :, None, None], values, 0).astype(jnp.int32)


def draw_block_source(key, part):
    group_blocks = GROUP // BLOCK
    sources = jax.random.randint(jax.random.fold_in(key, 37), (BLOCKS, SLOTS), 0, 3 * group_blocks)
    own_block = jnp.arange(BLOCKS) % group_blocks
    return sources.at[:, 0].set(own_block).astype(jnp.int32)


def touch_ends(values, key, low, top_value):
    extent = values.shape
    index_at = [jax.random.randint(jax.random.fold_in(key, axis), (), 0, extent[axis]) for axis in range(len(extent))]
    values = values.at[tuple(index_at)].set(low)
    longest = extent.index(max(extent))
    index_at[longest] = (index_at[longest] + 1) % extent[longest]
    return values.at[tuple(index_at)].set(top_value)


def shard_levels(rng, dims, cuts, low, top_value):
    factor_of = 1.0
    for dim, shards_of in cuts:
        steps = jax.random.uniform(jax.random.fold_in(jax.random.fold_in(rng, 6), dim), (shards_of,), jnp.float32, low / len(cuts), top_value / len(cuts))
        factor_of = factor_of * jnp.repeat(jnp.exp(steps), dims[dim] // shards_of).reshape((-1,) + (1,) * (len(dims) - 1 - dim))
    return factor_of


def bell_draw(own_key, shape, scale, reach, pieces=(), kind=jnp.bfloat16):
    gain = shard_levels(own_key, shape, pieces, -0.22, 0.18) if pieces else 1.0
    entries = jax.random.normal(own_key, shape, jnp.float32) * scale * gain
    return jnp.minimum(jnp.maximum(entries, -reach), reach).astype(kind)


def setup_inputs(seed: int = 0) -> dict:
    splits = jax.random.split(jax.random.key(seed), 7)
    return {
        "features": bell_draw(splits[0], (NODES, FEAT), 1.0, 6.0, ((0, 32),), jnp.float32),
        "self_weight": bell_draw(splits[1], (FEAT, CLASSES), FEAT ** -0.5, 0.375, (), jnp.float32),
        "neigh_weight": bell_draw(splits[2], (FEAT, CLASSES), 0.2, 1.2, (), jnp.float32),
        "block_source": draw_block_source(jax.random.fold_in(splits[6], 71), 0),
        "edge_weights": draw_edge_weights(jax.random.fold_in(splits[6], 71), 0),
        "labels": touch_ends(jax.random.randint(splits[5], (NODES,), 0, CLASSES), jax.random.fold_in(splits[5], 1), 0, CLASSES - 1).astype(jnp.int32),
    }


def reference(features, self_weight, neigh_weight, block_source, edge_weights, labels):
    high = lax.Precision.HIGHEST
    block_total = NODES // BLOCK
    block_count = ROWS_DEV // BLOCK
    group_blocks = GROUP // BLOCK
    device_total = NODES // ROWS_DEV
    lowered = lax.optimization_barrier(features.astype(jnp.bfloat16)).astype(jnp.float32)
    table = lowered.reshape(block_total, BLOCK, FEAT)
    device_ids = jnp.arange(device_total, dtype=jnp.int32)
    region = device_ids // N_REP
    region_row = region // N_COL
    region_col = region % N_COL
    peer_regions = jnp.stack([region, region_row * N_COL + (region_col - 1) % N_COL, region_row * N_COL + (region_col + 1) % N_COL], axis=1).astype(jnp.int32)
    source_dev = block_source.reshape(device_total, block_count, SLOTS).astype(jnp.int32)
    global_source = (peer_regions[device_ids[:, None, None], source_dev // group_blocks] * group_blocks + source_dev % group_blocks).astype(jnp.int32)
    weights_dev = edge_weights.reshape(device_total, block_count, SLOTS, BLOCK, BLOCK)
    degree = jnp.sum(edge_weights, axis=(1, 3)).astype(jnp.float32)

    def aggregate_device(inputs):
        weight_tiles, sources = inputs
        return jnp.einsum("bsij,bsjf->bif", weight_tiles.astype(jnp.float32), table[sources], precision=high)

    aggregated = lax.map(aggregate_device, (weights_dev, global_source))
    neighbour_mean = (aggregated.reshape(block_total, BLOCK, FEAT) / degree[..., None]).reshape(NODES, FEAT)
    logits = jnp.dot(features, self_weight, precision=high) + jnp.dot(neighbour_mean, neigh_weight, precision=high)
    target = (labels[:, None] == jnp.arange(CLASSES, dtype=jnp.int32)[None, :]).astype(jnp.float32)
    residual = jax.nn.sigmoid(logits) - target
    grad_self = jnp.dot(features.T, residual, precision=high)
    grad_neigh = jnp.dot(neighbour_mean.T, residual, precision=high)
    spread = jnp.dot(residual, neigh_weight.T, precision=high).reshape(block_total, BLOCK, FEAT) / degree[..., None]
    spread = lax.optimization_barrier(spread.astype(jnp.bfloat16)).astype(jnp.float32)
    spread_dev = spread.reshape(device_total, block_count, BLOCK, FEAT)

    def back_device(running, inputs):
        weight_tiles, sources, spread_rows, peers = inputs
        contrib = jnp.einsum("bsij,bif->bsjf", weight_tiles.astype(jnp.float32), spread_rows, precision=high)
        partial_sum = jnp.zeros((3 * group_blocks, BLOCK, FEAT), jnp.float32)
        partial_sum = partial_sum.at[sources.reshape(-1)].add(contrib.reshape(-1, BLOCK, FEAT))
        partial_sum = lax.optimization_barrier(partial_sum.astype(jnp.bfloat16)).astype(jnp.float32)
        target_blocks = (peers[:, None] * group_blocks + jnp.arange(group_blocks, dtype=jnp.int32)[None, :]).reshape(-1).astype(jnp.int32)
        return running.at[target_blocks].add(partial_sum), None

    returned, unused = lax.scan(back_device, jnp.zeros((block_total, BLOCK, FEAT), jnp.float32), (weights_dev, source_dev, spread_dev, peer_regions))
    grad_features = jnp.dot(residual, self_weight.T, precision=high) + returned.reshape(NODES, FEAT)
    return (grad_self, grad_neigh, grad_features)
```

```python
import functools

import jax
import jax.numpy as jnp
from jax import lax
from jax.experimental import pallas as pl
from jax.experimental.pallas import tpu as pltpu
from jax.sharding import PartitionSpec as P

BLOCK = 64
F32 = jnp.float32
BF16 = jnp.bfloat16
HIGH = lax.Precision.HIGHEST
VMEM = pl.BlockSpec(memory_space=pltpu.VMEM)
SMEM = pl.BlockSpec(memory_space=pltpu.SMEM)
ANY = pl.BlockSpec(memory_space=pl.ANY)


def shape(dims, dtype):
    return jax.ShapeDtypeStruct(dims, dtype)


def call(body, out_shape, operands, in_specs, out_specs, scratch=(), flops=0):
    moved = sum(x.size * x.dtype.itemsize for x in list(operands) + list(out_shape))
    return pl.pallas_call(
        body,
        out_shape=out_shape,
        in_specs=in_specs,
        out_specs=out_specs,
        scratch_shapes=scratch,
        compiler_params=pltpu.CompilerParams(vmem_limit_bytes=40 << 20),
        cost_estimate=pl.CostEstimate(flops=flops, bytes_accessed=moved, transcendentals=0),
    )(*operands)


def dot(a, b, contract=((1,), (0,)), precision=HIGH):
    return lax.dot_general(a, b, (contract, ((), ())), precision=precision, preferred_element_type=F32)


def prepare_body(edge_ref, feat_ref, self_ref, wide_ref, tall_ref, inverse_ref, logit_ref):
    blocks, slots = edge_ref.shape[:2]

    @pl.loop(0, blocks)
    def _(b):
        wide = jnp.concatenate([edge_ref[b, s].astype(F32) for s in range(slots)], axis=1)
        wide_ref[b] = wide.astype(BF16)
        tall_ref[b] = wide.T.astype(BF16)
        degree = jnp.sum(wide, axis=1, keepdims=True)
        inverse_ref[b] = jnp.broadcast_to(1.0 / degree, inverse_ref.shape[1:])

    logit_ref[...] = dot(feat_ref[...], self_ref[...])


def forward_body(*refs):
    pieces, refs = refs[:12], refs[12:]
    index_ref, wide_ref, inverse_ref, logit_ref, label_ref, feat_ref, neigh_ref = refs[:7]
    residual_ref, spread_ref, self_part_ref, neigh_part_ref, table, mean, sems = refs[7:]
    per = pieces[0].shape[0]
    copies = [
        pltpu.make_async_copy(piece, table.at[pl.ds(i * per, per)], sems.at[i])
        for i, piece in enumerate(pieces)
    ]
    for c in copies:
        c.start()
    for c in copies:
        c.wait()
    blocks, rows, wide_cols = wide_ref.shape
    slots = wide_cols // BLOCK
    width = mean.shape[1]

    @pl.loop(0, blocks)
    def _(b):
        gathered = jnp.concatenate([table[index_ref[b, s]] for s in range(slots)], axis=0)
        total = dot(wide_ref[b], gathered, precision=None)
        scale = jnp.concatenate([inverse_ref[b]] * (width // 128), axis=1)
        mean[pl.ds(pl.multiple_of(b * rows, rows), rows)] = total * scale

    logits = logit_ref[...] + dot(mean[...], neigh_ref[...])
    classes = lax.broadcasted_iota(jnp.int32, logits.shape, 1)
    target = jnp.where(classes == label_ref[...], 1.0, 0.0)
    residual = 1.0 / (1.0 + jnp.exp(-logits)) - target
    residual_ref[...] = residual
    spread = dot(residual, neigh_ref[...], ((1,), (1,)))
    inverse = inverse_ref[...].reshape(blocks * rows, 128)
    scale = jnp.concatenate([inverse] * (width // 128), axis=1)
    spread_ref[...] = (spread * scale).astype(BF16).reshape(spread_ref.shape)
    self_part_ref[...] = dot(feat_ref[...], residual, ((0,), (0,)))
    neigh_part_ref[...] = dot(mean[...], residual, ((0,), (0,)))


def backward_body(index_ref, spread_ref, tall_ref, send_ref, keep_ref, terms):
    blocks, tall_rows, _ = tall_ref.shape
    slots = tall_rows // BLOCK
    per = send_ref.shape[1]
    terms[...] = jnp.zeros_like(terms)

    @pl.loop(0, blocks)
    def _(b):
        contrib = dot(tall_ref[b], spread_ref[b], precision=None)
        for s in range(slots):
            at = index_ref[b, s]
            terms[at] = terms[at] + contrib[s * BLOCK : (s + 1) * BLOCK]

    for out_ref, core in ((keep_ref, 0), (send_ref, 1)):
        place = 0
        for rel in (2 + core, core):
            for region in (1, 2, 0):
                out_ref[place] = terms[pl.ds((region * 4 + rel) * per, per)].astype(BF16)
                place += 1


def chunk_body(groups, place_ref, mine_ref, got_ref, *outs):
    rows = mine_ref.shape[0] // groups
    for d, out in enumerate(outs):
        at = pl.ds(pl.multiple_of((place_ref[0] ^ d) * rows, rows), rows)
        out[...] = mine_ref[at] + got_ref[at]


def assemble_body(groups, place_ref, *refs):
    out = refs[-1]
    rows = out.shape[0] // groups
    for d, chunk in enumerate(refs[:-1]):
        at = pl.ds(pl.multiple_of((place_ref[0] ^ d) * rows, rows), rows)
        out[at] = chunk[...]


def tree_sum(values):
    values = list(values)
    while len(values) > 1:
        values = [a + b for a, b in zip(values[0::2], values[1::2])]
    return values[0]


def on_device(features, self_weight, neigh_weight, block_source, edge_weights, labels):
    rows, width = features.shape
    blocks, slots = block_source.shape
    classes = self_weight.shape[1]
    cols, reps, lines = lax.axis_size("col"), lax.axis_size("rep"), lax.axis_size("row")
    assert reps == 4
    me = lax.axis_index("rep")

    def core_swap(x):
        return lax.ppermute(x, "rep", [(i, i ^ 1) for i in range(reps)])

    def half_swap(x):
        return lax.ppermute(x, "rep", [(i, i ^ 2) for i in range(reps)])

    def up(x):
        return lax.ppermute(x, "col", [(i, (i + 1) % cols) for i in range(cols)])

    def down(x):
        return lax.ppermute(x, "col", [((i + 1) % cols, i) for i in range(cols)])

    own = features.astype(BF16).reshape(blocks, BLOCK, width)
    half, lower, upper, core = half_swap(own), up(own), down(own), core_swap(own)
    lower_half, upper_half = half_swap(lower), half_swap(upper)
    pieces = [
        own, core, half, core_swap(half),
        lower, core_swap(lower), lower_half, core_swap(lower_half),
        upper, core_swap(upper), upper_half, core_swap(upper_half),
    ]

    group_blocks = reps * blocks
    region, inner = block_source // group_blocks, block_source % group_blocks
    index = (region * reps + ((inner // blocks) ^ me)) * blocks + inner % blocks

    wide_cols = slots * BLOCK
    wide, tall, inverse, self_logits = call(
        prepare_body,
        (
            shape((blocks, BLOCK, wide_cols), BF16),
            shape((blocks, wide_cols, BLOCK), BF16),
            shape((blocks, BLOCK, 128), F32),
            shape((rows, classes), F32),
        ),
        (edge_weights, features, self_weight),
        [VMEM] * 3,
        [VMEM] * 4,
        flops=12 * rows * width * classes,
    )
    residual, spread, self_part, neigh_part = call(
        forward_body,
        (
            shape((rows, classes), F32),
            shape((blocks, BLOCK, width), BF16),
            shape((width, classes), F32),
            shape((width, classes), F32),
        ),
        (*pieces, index, wide, inverse, self_logits, labels.reshape(rows, 1), features, neigh_weight),
        [ANY] * 12 + [SMEM] + [VMEM] * 6,
        [VMEM] * 4,
        scratch=[
            pltpu.VMEM((12 * blocks, BLOCK, width), BF16),
            pltpu.VMEM((rows, width), F32),
            pltpu.SemaphoreType.DMA((12,)),
        ],
        flops=60 * rows * width * classes,
    )

    first = me % 2 == 0
    kept = jnp.where(first, self_part, neigh_part)
    got = core_swap(jnp.where(first, neigh_part, self_part))

    send, keep = call(
        backward_body,
        (shape((6, blocks, BLOCK, width), BF16), shape((6, blocks, BLOCK, width), BF16)),
        (index, spread, tall),
        [SMEM] + [VMEM] * 2,
        [VMEM] * 2,
        scratch=[pltpu.VMEM((12 * blocks, BLOCK, width), F32)],
        flops=2 * rows * wide_cols * width,
    )
    arrived = core_swap(send)

    groups = lines * reps // 2
    place = (lax.axis_index("row") * (reps // 2) + me // 2).astype(jnp.int32)

    def to_group(x, d):
        pairs = []
        for g in range(groups):
            for c in range(2):
                h = g ^ d
                pairs.append((g * 2 + c, h * 2 + c))
        return lax.ppermute(x, ("row", "rep"), pairs)

    chunk = shape((width // groups, classes), F32)
    chunks = call(
        functools.partial(chunk_body, groups),
        (chunk,) * groups,
        (place.reshape(1), kept, got),
        [SMEM, VMEM, VMEM],
        [VMEM] * groups,
    )
    mine = tree_sum([chunks[0]] + [to_group(chunks[d], d) for d in range(1, groups)])

    def both(a, b):
        return a.astype(F32) + b.astype(F32)

    half_near = half_swap(both(keep[0:2], arrived[0:2]).astype(BF16))
    half_own = half_swap(both(keep[2], arrived[2]).astype(BF16))

    def to_col(x, d):
        return lax.ppermute(x, "col", [(i, i ^ d) for i in range(cols)])

    mine = tree_sum([mine] + [to_col(mine, d) for d in range(1, cols)])

    near = both(keep[3:5], arrived[3:5]) + half_near.astype(F32)
    from_upper = down(near[0].astype(BF16))
    from_lower = up(near[1].astype(BF16))

    parts = [mine] + [to_group(mine, d) for d in range(1, groups)]
    (whole,) = call(
        functools.partial(assemble_body, groups),
        (shape((width, classes), F32),),
        (place.reshape(1), *parts),
        [SMEM] + [VMEM] * groups,
        [VMEM],
    )
    other = core_swap(whole)
    grad_self = jnp.where(first, whole, other)
    grad_neigh = jnp.where(first, other, whole)

    direct = jnp.dot(residual, self_weight.T, precision=HIGH)
    own_terms = both(keep[5], arrived[5]) + half_own.astype(F32)
    own_terms = own_terms + from_upper.astype(F32) + from_lower.astype(F32)
    grad_features = direct + own_terms.reshape(rows, width)
    return grad_self, grad_neigh, grad_features


def solution(mesh):
    split = ("row", "col", "rep")
    return jax.shard_map(
        on_device,
        mesh=mesh,
        in_specs=(P(split, None), P(), P(), P(split, None), P(split, None, None, None), P(split)),
        out_specs=(P(), P(), P(split, None)),
        check_vma=False,
    )
```

```python
import functools

import jax
import jax.numpy as jnp
from jax import lax
from jax.experimental import pallas as pl
from jax.experimental.pallas import tpu as pltpu
from jax.sharding import PartitionSpec as P

BLOCK = 64
F32 = jnp.float32
BF16 = jnp.bfloat16
VMEM = pl.BlockSpec(memory_space=pltpu.VMEM)
SMEM = pl.BlockSpec(memory_space=pltpu.SMEM)
ANY = pl.BlockSpec(memory_space=pl.ANY)
ROWS_BOTH = ((0,), (0,))


def shape(dims, dtype):
    return jax.ShapeDtypeStruct(dims, dtype)


def call(body, out_shape, operands, in_specs, out_specs, scratch=(), flops=0, vmem=60):
    moved = sum(x.size * x.dtype.itemsize for x in list(operands) + list(out_shape))
    return pl.pallas_call(
        body,
        out_shape=out_shape,
        in_specs=in_specs,
        out_specs=out_specs,
        scratch_shapes=scratch,
        compiler_params=pltpu.CompilerParams(vmem_limit_bytes=vmem << 20),
        cost_estimate=pl.CostEstimate(flops=flops, bytes_accessed=moved, transcendentals=0),
    )(*operands)


def dot(a, b, contract=((1,), (0,))):
    return lax.dot_general(a, b, (contract, ((), ())), preferred_element_type=F32)


def halves(x):
    high = x.astype(BF16)
    return high, (x - high.astype(F32)).astype(BF16)


def dot3(a, b, contract=((1,), (0,))):
    return dot(a[0], b[0], contract) + (dot(a[0], b[1], contract) + dot(a[1], b[0], contract))


def wider(x):
    return jnp.concatenate([x, x], axis=-1)


def prepare_body(
    edge_hbm, feat_hbm, self_hbm, neigh_hbm, label_ref,
    wide_ref, tall_ref, inverse_ref, logit_ref, label_out, feat_out, weight_out,
    edge_ref, feat_ref, self_ref, neigh_ref, sems,
):
    blocks, slots = edge_ref.shape[:2]
    tiles = [pltpu.make_async_copy(edge_hbm.at[b], edge_ref.at[b], sems.at[b]) for b in range(blocks)]
    dense = [
        pltpu.make_async_copy(source, target, sems.at[blocks + i])
        for i, (source, target) in enumerate(
            ((feat_hbm, feat_ref), (self_hbm, self_ref), (neigh_hbm, neigh_ref))
        )
    ]
    for c in tiles + dense:
        c.start()
    lines = label_ref.shape[0]
    columns = jnp.concatenate([label_ref[...].astype(F32), jnp.zeros((8 - lines % 8, 128), F32)], axis=0).T
    for r in range(lines):
        label_out[r * 128 : (r + 1) * 128] = jnp.broadcast_to(columns[:, r : r + 1], (128, 128))
    for b in range(blocks):
        tiles[b].wait()
        wide = jnp.concatenate([edge_ref[b, s].astype(F32) for s in range(slots)], axis=1)
        wide_ref[b] = wide.astype(BF16)
        tall_ref[b] = wide.T.astype(BF16)
        degree = jnp.sum(wide, axis=1, keepdims=True)
        inverse_ref[b] = jnp.broadcast_to(1.0 / degree, inverse_ref.shape[1:])
    for c in dense:
        c.wait()
    feat, own, neigh = feat_ref[...], self_ref[...], neigh_ref[...]
    logit_ref[...] = dot3(halves(feat), halves(own))
    for k, x in enumerate(halves(feat.T)):
        feat_out[k] = x
    for k, x in enumerate(halves(neigh) + halves(neigh.T) + halves(own.T)):
        weight_out[k] = x


def layer_body(*refs):
    pieces, refs = refs[:12], refs[12:]
    place_ref, source_ref, refs = refs[0], refs[1], refs[2:]
    inputs, outputs, refs = refs[:7], refs[7:14], refs[14:]
    table, held, made, refs = refs[0], refs[1:8], refs[8:15], refs[15:]
    mean, terms, index, piece_sems, in_sems, out_sems = refs
    wide_ref, inverse_ref, logit_ref, label_ref, weight_ref, tall_ref, feat_ref = held
    direct_ref, mine_ref, passed_ref = made[4:]
    per = pieces[0].shape[0]
    copies = [
        pltpu.make_async_copy(piece, table.at[pl.ds(i * per, per)], piece_sems.at[i])
        for i, piece in enumerate(pieces)
    ]
    loads = [pltpu.make_async_copy(x, y, in_sems.at[i]) for i, (x, y) in enumerate(zip(inputs, held))]
    for c in loads[:1] + copies + loads[1:]:
        c.start()

    def store(i, source, target):
        c = pltpu.make_async_copy(source, target, out_sems.at[i])
        c.start()
        return c

    blocks, rows, wide_cols = wide_ref.shape
    slots = wide_cols // BLOCK
    me = place_ref[0]

    for b in range(blocks):
        for s in range(slots):
            index[b, s] = source_ref[b, s] ^ (me * blocks)
    terms[...] = jnp.zeros_like(terms)
    for c in loads[:1] + copies + loads[1:2]:
        c.wait()

    for b in range(blocks):
        gathered = jnp.concatenate([table[index[b, s]] for s in range(slots)], axis=0)
        total = dot(wide_ref[b], gathered)
        mean[b * rows : (b + 1) * rows] = total * wider(inverse_ref[b])

    for c in loads[2:5]:
        c.wait()
    neigh, neigh_t, own_t = [(weight_ref[2 * k], weight_ref[2 * k + 1]) for k in range(3)]
    mean_parts = halves(mean[...])
    logits = logit_ref[...] + dot3(mean_parts, neigh)
    classes = lax.broadcasted_iota(jnp.int32, logits.shape, 1).astype(F32)
    target = jnp.where(classes == wider(label_ref[...]), 1.0, 0.0)
    residual = halves(1.0 / (1.0 + jnp.exp(-logits)) - target)
    inverse = inverse_ref[...].reshape(blocks * rows, 128)
    spread = (dot3(residual, neigh_t) * wider(inverse)).astype(BF16)
    direct_ref[...] = dot3(residual, own_t)
    stores = [store(0, direct_ref, outputs[4])]

    for c in loads[5:]:
        c.wait()
    for b in range(blocks):
        contrib = dot(tall_ref[b], spread[b * rows : (b + 1) * rows])
        for s in range(slots):
            at = index[b, s]
            terms[at] = terms[at] + contrib[s * BLOCK : (s + 1) * BLOCK]

    count = 1
    for core in (1, 0):
        for place in range(6):
            rel = 2 + core if place < 3 else core
            region = (1, 2, 0)[place % 3]
            which, at = (2 * core, place) if place < 2 else (2 * core + 1, place - 2)
            made[which][at] = terms[pl.ds((region * 4 + rel) * per, per)].astype(BF16)
            stores.append(store(count, made[which].at[at], outputs[which].at[at]))
            count += 1

    self_part = dot3((feat_ref[0], feat_ref[1]), residual)
    neigh_part = dot3(mean_parts, residual, ROWS_BOTH)
    first = me % 2 == 0
    mine_ref[...] = jnp.where(first, self_part, neigh_part)
    passed_ref[...] = jnp.where(first, neigh_part, self_part)
    stores.append(store(count, mine_ref, outputs[5]))
    stores.append(store(count + 1, passed_ref, outputs[6]))
    for c in stores:
        c.wait()


def split_body(place_ref, *refs):
    outs = [r for r in refs if r.shape != refs[0].shape]
    total = tree_sum(r[...] for r in refs[: len(refs) - len(outs)])
    chunks = total.reshape(len(outs), *outs[0].shape)
    if len(outs) == 1:
        outs[0][...] = chunks[0]
        return
    for d, out in enumerate(outs):
        for c in range(len(outs)):

            @pl.when(place_ref[0] ^ d == c)
            def _():
                out[...] = chunks[c]


def join_body(place_ref, *refs):
    out = refs[-1]
    rows = refs[0].shape[0]
    for d, chunk in enumerate(refs[:-1]):
        for c in range(len(refs) - 1):

            @pl.when(place_ref[0] ^ d == c)
            def _():
                out[c * rows : (c + 1) * rows] = chunk[...]


def tree_sum(values):
    values = list(values)
    while len(values) > 1:
        values = [sum(values[i + 1 : i + 2], values[i]) for i in range(0, len(values), 2)]
    return values[0]


def on_device(features, self_weight, neigh_weight, block_source, edge_weights, labels):
    rows, width = features.shape
    blocks, slots = block_source.shape
    classes = self_weight.shape[1]
    reps = lax.axis_size("rep")
    assert reps == 4
    me = lax.axis_index("rep").astype(jnp.int32)

    def swap(x, axis, d):
        return lax.ppermute(x, axis, [(i, i ^ d) for i in range(lax.axis_size(axis))])

    def core_swap(x):
        return swap(x, "rep", 1)

    def half_swap(x):
        return swap(x, "rep", 2)

    def up(x):
        cols = lax.axis_size("col")
        return lax.ppermute(x, "col", [(i, (i + 1) % cols) for i in range(cols)])

    def down(x):
        cols = lax.axis_size("col")
        return lax.ppermute(x, "col", [((i + 1) % cols, i) for i in range(cols)])

    own = features.astype(BF16).reshape(blocks, BLOCK, width)
    half, lower, upper, core = half_swap(own), up(own), down(own), core_swap(own)

    wide_cols = slots * BLOCK
    prepared = call(
        prepare_body,
        (
            shape((blocks, BLOCK, wide_cols), BF16),
            shape((blocks, wide_cols, BLOCK), BF16),
            shape((blocks, BLOCK, 128), F32),
            shape((rows, classes), F32),
            shape((rows, 128), F32),
            shape((2, width, rows), BF16),
            shape((6, width, classes), BF16),
        ),
        (edge_weights, features, self_weight, neigh_weight, labels.reshape(rows // 128, 128)),
        [ANY] * 4 + [VMEM],
        [VMEM] * 7,
        scratch=[
            pltpu.VMEM(edge_weights.shape, jnp.int32),
            pltpu.VMEM(features.shape, F32),
            pltpu.VMEM(self_weight.shape, F32),
            pltpu.VMEM(neigh_weight.shape, F32),
            pltpu.SemaphoreType.DMA((blocks + 3,)),
        ],
        flops=6 * rows * width * classes,
    )
    wide, tall, inverse, self_logits, label_cols, feat_parts, weight_parts = prepared
    half, lower, upper, core = (lax.optimization_barrier((x, inverse))[0] for x in (half, lower, upper, core))
    lower_half, upper_half = half_swap(lower), half_swap(upper)
    pieces = [
        own, core, half, core_swap(half),
        lower, core_swap(lower), lower_half, core_swap(lower_half),
        upper, core_swap(upper), upper_half, core_swap(upper_half),
    ]

    def piece_shape(*lead):
        return shape((*lead, blocks, BLOCK, width), BF16)

    inputs = (wide, inverse, self_logits, label_cols, weight_parts, tall, feat_parts)
    outputs = (
        piece_shape(2), piece_shape(4), piece_shape(2), piece_shape(4),
        shape((rows, width), F32), shape((width, classes), F32), shape((width, classes), F32),
    )
    keep_near, keep_rest, send_near, send_rest, direct, mine, passed = call(
        layer_body,
        outputs,
        (*pieces, me.reshape(1), block_source, *inputs),
        [ANY] * 12 + [SMEM] * 2 + [ANY] * 7,
        [ANY] * 7,
        scratch=[
            pltpu.VMEM((12 * blocks, BLOCK, width), BF16),
            *[pltpu.VMEM(x.shape, x.dtype) for x in inputs + outputs],
            pltpu.VMEM((rows, width), F32),
            pltpu.VMEM((12 * blocks, BLOCK, width), F32),
            pltpu.SMEM((blocks, slots), jnp.int32),
            pltpu.SemaphoreType.DMA((12,)),
            pltpu.SemaphoreType.DMA((7,)),
            pltpu.SemaphoreType.DMA((15,)),
        ],
        flops=40 * rows * width * classes,
    )
    got_near, got_rest, got = core_swap(send_near), core_swap(send_rest), core_swap(passed)

    def both(a, b):
        return a.astype(F32) + b.astype(F32)

    lines, cols = lax.axis_size("row"), lax.axis_size("col")
    group = lines * reps // 2
    place = lax.axis_index("row").astype(jnp.int32) * (reps // 2) + me // 2

    def to_group(x, d):
        pairs = [(g * 2 + c, (g ^ d) * 2 + c) for g in range(group) for c in range(2)]
        return lax.ppermute(x, ("row", "rep"), pairs)

    def split(parts):
        chunk = shape((parts[0].shape[0] // group, classes), F32)
        return call(
            split_body,
            (chunk,) * group,
            (place.reshape(1), *parts),
            [SMEM] + [VMEM] * len(parts),
            [VMEM] * group,
            vmem=4,
        )

    def join(chunk):
        parts = [chunk] + [to_group(chunk, d) for d in range(1, group)]
        (out,) = call(
            join_body,
            (shape((chunk.shape[0] * group, classes), F32),),
            (place.reshape(1), *parts),
            [SMEM] + [VMEM] * group,
            [VMEM],
            vmem=4,
        )
        return out

    near = [both(keep_near[k], got_near[k]).astype(BF16) for k in range(2)]
    near, got = lax.optimization_barrier((near, got))
    half_near = [half_swap(x) for x in near]
    chunks = split((mine, got))
    part = tree_sum([chunks[0]] + [to_group(c, d) for d, c in enumerate(chunks) if d])
    step = 1
    while step < cols:
        part = part + swap(part, "col", step)
        step *= 2
    half_near, part, got_rest = lax.optimization_barrier((half_near, part, got_rest))

    near = [both(keep_rest[1 + k], got_rest[1 + k]) + half_near[k].astype(F32) for k in range(2)]
    from_upper = down(near[0].astype(BF16))
    from_lower = up(near[1].astype(BF16))
    half_own = half_swap(both(keep_rest[0], got_rest[0]).astype(BF16))
    whole = join(part)
    other = core_swap(whole)
    first = me % 2 == 0
    grad_self = jnp.where(first, whole, other)
    grad_neigh = jnp.where(first, other, whole)

    own_terms = both(keep_rest[3], got_rest[3]) + half_own.astype(F32)
    own_terms = own_terms + from_upper.astype(F32) + from_lower.astype(F32)
    grad_features = direct + own_terms.reshape(rows, width)
    return grad_self, grad_neigh, grad_features


def solution(mesh):
    split = ("row", "col", "rep")
    return jax.shard_map(
        on_device,
        mesh=mesh,
        in_specs=(P(split, None), P(), P(), P(split, None), P(split, None, None, None), P(split)),
        out_specs=(P(), P(), P(split, None)),
        check_vma=False,
    )
```

```python
import functools

import jax
import jax.numpy as jnp
from jax import lax
from jax.experimental import pallas as pl
from jax.experimental.pallas import tpu as pltpu
from jax.sharding import PartitionSpec as P

BLOCK = 64
F32 = jnp.float32
BF16 = jnp.bfloat16
VMEM = pl.BlockSpec(memory_space=pltpu.VMEM)
SMEM = pl.BlockSpec(memory_space=pltpu.SMEM)
ANY = pl.BlockSpec(memory_space=pl.ANY)
ROWS_BOTH = ((0,), (0,))


def shape(dims, dtype):
    return jax.ShapeDtypeStruct(dims, dtype)


def call(body, out_shape, operands, in_specs, out_specs, scratch=(), flops=0, vmem=60):
    moved = sum(x.size * x.dtype.itemsize for x in list(operands) + list(out_shape))
    return pl.pallas_call(
        body,
        out_shape=out_shape,
        in_specs=in_specs,
        out_specs=out_specs,
        scratch_shapes=scratch,
        compiler_params=pltpu.CompilerParams(vmem_limit_bytes=vmem << 20),
        cost_estimate=pl.CostEstimate(flops=flops, bytes_accessed=moved, transcendentals=0),
    )(*operands)


def dot(a, b, contract=((1,), (0,))):
    return lax.dot_general(a, b, (contract, ((), ())), preferred_element_type=F32)


def halves(x):
    high = x.astype(BF16)
    return high, (x - high.astype(F32)).astype(BF16)


def dot3(a, b, contract=((1,), (0,))):
    return dot(a[0], b[0], contract) + (dot(a[0], b[1], contract) + dot(a[1], b[0], contract))


def wider(x):
    return jnp.concatenate([x, x], axis=-1)


def prepare_body(
    edge_hbm, feat_hbm, self_hbm, neigh_hbm, label_ref,
    wide_ref, inverse_ref, logit_ref, label_out, feat_out, weight_out,
    edge_ref, feat_ref, self_ref, neigh_ref, sems,
):
    blocks, slots = edge_ref.shape[:2]
    tiles = [pltpu.make_async_copy(edge_hbm.at[b], edge_ref.at[b], sems.at[b]) for b in range(blocks)]
    dense = [
        pltpu.make_async_copy(source, target, sems.at[blocks + i])
        for i, (source, target) in enumerate(
            ((feat_hbm, feat_ref), (self_hbm, self_ref), (neigh_hbm, neigh_ref))
        )
    ]
    for c in tiles + dense:
        c.start()
    lines = label_ref.shape[0]
    columns = jnp.concatenate([label_ref[...].astype(F32), jnp.zeros((8 - lines % 8, 128), F32)], axis=0).T
    for r in range(lines):
        label_out[r * 128 : (r + 1) * 128] = jnp.broadcast_to(columns[:, r : r + 1], (128, 128)).astype(BF16)
    for b in range(blocks):
        tiles[b].wait()
        wide = jnp.concatenate([edge_ref[b, s].astype(F32) for s in range(slots)], axis=1)
        wide_ref[b] = wide.astype(BF16)
        degree = jnp.sum(wide, axis=1, keepdims=True)
        inverse_ref[b] = jnp.broadcast_to(1.0 / degree, inverse_ref.shape[1:])
    for c in dense:
        c.wait()
    feat, own, neigh = feat_ref[...], self_ref[...], neigh_ref[...]
    logit_ref[...] = dot3(halves(feat), halves(own))
    for k, x in enumerate(halves(feat.T)):
        feat_out[k] = x
    for k, x in enumerate(halves(neigh) + halves(neigh.T) + halves(own.T)):
        weight_out[k] = x


def layer_body(*refs):
    pieces, refs = refs[:12], refs[12:]
    source_hbm, refs = refs[0], refs[1:]
    inputs, outputs, refs = refs[:6], refs[6:13], refs[13:]
    table, held, made, refs = refs[0], refs[1:7], refs[7:14], refs[14:]
    mean, terms, source_ref, source_sem, piece_sems, in_sems, out_sems = refs
    sources = pltpu.make_async_copy(source_hbm, source_ref, source_sem)
    sources.start()
    wide_ref, inverse_ref, logit_ref, label_ref, weight_ref, feat_ref = held
    direct_ref, mine_ref, passed_ref = made[4:]
    per = pieces[0].shape[0]
    copies = [
        pltpu.make_async_copy(piece, table.at[pl.ds(i * per, per)], piece_sems.at[i])
        for i, piece in enumerate(pieces)
    ]
    loads = [pltpu.make_async_copy(x, y, in_sems.at[i]) for i, (x, y) in enumerate(zip(inputs, held))]
    for c in loads[:1] + copies + loads[1:]:
        c.start()

    def store(i, source, target):
        c = pltpu.make_async_copy(source, target, out_sems.at[i])
        c.start()
        return c

    blocks, rows, wide_cols = wide_ref.shape
    slots = wide_cols // BLOCK
    me = lax.axis_index("rep")

    def named(b, s):
        return source_ref[b, s] ^ (me * blocks)

    terms[...] = jnp.zeros_like(terms)
    for c in [sources] + loads[:1] + copies + loads[1:2]:
        c.wait()

    for b in range(blocks):
        gathered = jnp.concatenate([table[named(b, s)] for s in range(slots)], axis=0)
        total = dot(wide_ref[b], gathered)
        mean[b * rows : (b + 1) * rows] = total * wider(inverse_ref[b])

    for c in loads[2:5]:
        c.wait()
    neigh, neigh_t, own_t = [(weight_ref[2 * k], weight_ref[2 * k + 1]) for k in range(3)]
    mean_parts = halves(mean[...])
    logits = logit_ref[...] + dot3(mean_parts, neigh)
    classes = lax.broadcasted_iota(jnp.int32, logits.shape, 1).astype(F32)
    target = jnp.where(classes == wider(label_ref[...].astype(F32)), 1.0, 0.0)
    residual = halves(1.0 / (1.0 + jnp.exp(-logits)) - target)
    inverse = inverse_ref[...].reshape(blocks * rows, 128)
    spread = (dot3(residual, neigh_t) * wider(inverse)).astype(BF16)
    direct_ref[...] = dot3(residual, own_t)
    stores = [store(0, direct_ref, outputs[4])]

    for c in loads[5:]:
        c.wait()
    for b in range(blocks):
        contrib = dot(wide_ref[b], spread[b * rows : (b + 1) * rows], ROWS_BOTH)
        for s in range(slots):
            at = named(b, s)
            terms[at] = terms[at] + contrib[s * BLOCK : (s + 1) * BLOCK]

    count = 1
    for core in (1, 0):
        for place in range(6):
            rel = 2 + core if place < 3 else core
            region = (1, 2, 0)[place % 3]
            which, at = (2 * core, place) if place < 2 else (2 * core + 1, place - 2)
            made[which][at] = terms[pl.ds((region * 4 + rel) * per, per)].astype(BF16)
            stores.append(store(count, made[which].at[at], outputs[which].at[at]))
            count += 1

    self_part = dot3((feat_ref[0], feat_ref[1]), residual)
    neigh_part = dot3(mean_parts, residual, ROWS_BOTH)
    first = me % 2 == 0
    mine_ref[...] = jnp.where(first, self_part, neigh_part)
    passed_ref[...] = jnp.where(first, neigh_part, self_part)
    stores.append(store(count, mine_ref, outputs[5]))
    stores.append(store(count + 1, passed_ref, outputs[6]))
    for c in stores:
        c.wait()


def own_body(direct_ref, keep_ref, got_ref, out_ref):
    out_ref[...] = direct_ref[...] + (keep_ref[3].astype(F32) + got_ref[3].astype(F32))


def split_body(place_ref, *refs):
    outs = [r for r in refs if r.shape != refs[0].shape]
    total = tree_sum(r[...] for r in refs[: len(refs) - len(outs)])
    chunks = total.reshape(len(outs), *outs[0].shape)
    if len(outs) == 1:
        outs[0][...] = chunks[0]
        return
    for d, out in enumerate(outs):
        for c in range(len(outs)):

            @pl.when(place_ref[0] ^ d == c)
            def _():
                out[...] = chunks[c]


def join_body(place_ref, *refs):
    out = refs[-1]
    rows = refs[0].shape[0]
    for d, chunk in enumerate(refs[:-1]):
        for c in range(len(refs) - 1):

            @pl.when(place_ref[0] ^ d == c)
            def _():
                out[c * rows : (c + 1) * rows] = chunk[...]


def tree_sum(values):
    values = list(values)
    while len(values) > 1:
        values = [sum(values[i + 1 : i + 2], values[i]) for i in range(0, len(values), 2)]
    return values[0]


def on_device(features, self_weight, neigh_weight, block_source, edge_weights, labels):
    rows, width = features.shape
    blocks, slots = block_source.shape
    classes = self_weight.shape[1]
    reps = lax.axis_size("rep")
    assert reps == 4
    me = lax.axis_index("rep").astype(jnp.int32)

    def swap(x, axis, d):
        return lax.ppermute(x, axis, [(i, i ^ d) for i in range(lax.axis_size(axis))])

    def core_swap(x):
        return swap(x, "rep", 1)

    def half_swap(x):
        return swap(x, "rep", 2)

    def up(x):
        cols = lax.axis_size("col")
        return lax.ppermute(x, "col", [(i, (i + 1) % cols) for i in range(cols)])

    def down(x):
        cols = lax.axis_size("col")
        return lax.ppermute(x, "col", [((i + 1) % cols, i) for i in range(cols)])

    own = features.astype(BF16).reshape(blocks, BLOCK, width)
    half, lower, upper, core = half_swap(own), up(own), down(own), core_swap(own)

    wide_cols = slots * BLOCK
    prepared = call(
        prepare_body,
        (
            shape((blocks, BLOCK, wide_cols), BF16),
            shape((blocks, BLOCK, 128), F32),
            shape((rows, classes), F32),
            shape((rows, 128), BF16),
            shape((2, width, rows), BF16),
            shape((6, width, classes), BF16),
        ),
        (edge_weights, features, self_weight, neigh_weight, labels.reshape(rows // 128, 128)),
        [ANY] * 4 + [VMEM],
        [VMEM] * 6,
        scratch=[
            pltpu.VMEM(edge_weights.shape, jnp.int32),
            pltpu.VMEM(features.shape, F32),
            pltpu.VMEM(self_weight.shape, F32),
            pltpu.VMEM(neigh_weight.shape, F32),
            pltpu.SemaphoreType.DMA((blocks + 3,)),
        ],
        flops=6 * rows * width * classes,
    )
    wide, inverse, self_logits, label_cols, feat_parts, weight_parts = prepared
    half, lower, upper, core = (lax.optimization_barrier((x, inverse))[0] for x in (half, lower, upper, core))
    lower_half, upper_half = half_swap(lower), half_swap(upper)
    pieces = [
        own, core, half, core_swap(half),
        lower, core_swap(lower), lower_half, core_swap(lower_half),
        upper, core_swap(upper), upper_half, core_swap(upper_half),
    ]

    def piece_shape(*lead):
        return shape((*lead, blocks, BLOCK, width), BF16)

    inputs = (wide, inverse, self_logits, label_cols, weight_parts, feat_parts)
    outputs = (
        piece_shape(2), piece_shape(4), piece_shape(2), piece_shape(4),
        shape((rows, width), F32), shape((width, classes), F32), shape((width, classes), F32),
    )
    keep_near, keep_rest, send_near, send_rest, direct, mine, passed = call(
        layer_body,
        outputs,
        (*pieces, block_source, *inputs),
        [ANY] * 19,
        [ANY] * 7,
        scratch=[
            pltpu.VMEM((12 * blocks, BLOCK, width), BF16),
            *[pltpu.VMEM(x.shape, x.dtype) for x in inputs + outputs],
            pltpu.VMEM((rows, width), F32),
            pltpu.VMEM((12 * blocks, BLOCK, width), F32),
            pltpu.SMEM((blocks, slots), jnp.int32),
            pltpu.SemaphoreType.DMA(()),
            pltpu.SemaphoreType.DMA((12,)),
            pltpu.SemaphoreType.DMA((6,)),
            pltpu.SemaphoreType.DMA((15,)),
        ],
        flops=40 * rows * width * classes,
    )
    got_near, got_rest, got = core_swap(send_near), core_swap(send_rest), core_swap(passed)

    def both(a, b):
        return a.astype(F32) + b.astype(F32)

    lines, cols = lax.axis_size("row"), lax.axis_size("col")
    line = lax.axis_index("row").astype(jnp.int32).reshape(1)

    def split(parts):
        chunk = shape((parts[0].shape[0] // lines, classes), F32)
        return call(
            split_body,
            (chunk,) * lines,
            (line, *parts),
            [SMEM] + [VMEM] * len(parts),
            [VMEM] * lines,
            vmem=4,
        )

    def join(chunk):
        parts = [chunk] + [swap(chunk, "row", d) for d in range(1, lines)]
        (out,) = call(
            join_body,
            (shape((chunk.shape[0] * lines, classes), F32),),
            (line, *parts),
            [SMEM] + [VMEM] * lines,
            [VMEM],
            vmem=4,
        )
        return out

    def together(*values):
        return lax.optimization_barrier(values)

    near, got = together(both(keep_near, got_near).astype(BF16), got)
    half_near = half_swap(near)
    chunks = split((mine, got))
    part = tree_sum([chunks[0]] + [swap(c.astype(BF16), "row", d).astype(F32) for d, c in enumerate(chunks) if d])
    step = 1
    while step < cols:
        part = part + swap(part, "col", step)
        step *= 2
    half_near, part, got_rest = together(half_near, part, got_rest)

    near = [both(keep_rest[1 + k], got_rest[1 + k]) + half_near[k].astype(F32) for k in range(2)]
    from_upper = down(near[0].astype(BF16))
    from_lower = up(near[1].astype(BF16))
    part = part + half_swap(part)
    whole = join(part)
    half_own = half_swap(both(keep_rest[0], got_rest[0]).astype(BF16))
    other = core_swap(whole)
    first = me % 2 == 0
    grad_self = jnp.where(first, whole, other)
    grad_neigh = jnp.where(first, other, whole)

    (own_terms,) = call(
        own_body,
        (shape((blocks, BLOCK, width), F32),),
        (direct.reshape(blocks, BLOCK, width), keep_rest, got_rest),
        [VMEM] * 3,
        [VMEM],
    )
    grad_features = own_terms + half_own.astype(F32) + both(from_upper, from_lower)
    return grad_self, grad_neigh, grad_features.reshape(rows, width)


def solution(mesh):
    split = ("row", "col", "rep")
    return jax.shard_map(
        on_device,
        mesh=mesh,
        in_specs=(P(split, None), P(), P(), P(split, None), P(split, None, None, None), P(split)),
        out_specs=(P(), P(), P(split, None)),
        check_vma=False,
    )
```

```python
import functools

import jax
import jax.numpy as jnp
from jax import lax
from jax.experimental import pallas as pl
from jax.experimental.pallas import tpu as pltpu
from jax.sharding import PartitionSpec as P

BLOCK = 64
F32 = jnp.float32
BF16 = jnp.bfloat16
VMEM = pl.BlockSpec(memory_space=pltpu.VMEM)
SMEM = pl.BlockSpec(memory_space=pltpu.SMEM)
ANY = pl.BlockSpec(memory_space=pl.ANY)
ROWS_BOTH = ((0,), (0,))


def shape(dims, dtype):
    return jax.ShapeDtypeStruct(dims, dtype)


def call(body, out_shape, operands, in_specs, out_specs, scratch=(), flops=0, vmem=60):
    moved = sum(x.size * x.dtype.itemsize for x in list(operands) + list(out_shape)) if flops else 0
    return pl.pallas_call(
        body,
        out_shape=out_shape,
        in_specs=in_specs,
        out_specs=out_specs,
        scratch_shapes=scratch,
        compiler_params=pltpu.CompilerParams(vmem_limit_bytes=vmem << 20),
        cost_estimate=pl.CostEstimate(flops=flops, bytes_accessed=moved, transcendentals=0),
    )(*operands)


def dot(a, b, contract=((1,), (0,))):
    return lax.dot_general(a, b, (contract, ((), ())), preferred_element_type=F32)


def halves(x):
    high = x.astype(BF16)
    return high, (x - high.astype(F32)).astype(BF16)


def dot3(a, b, contract=((1,), (0,))):
    return dot(a[0], b[0], contract) + (dot(a[0], b[1], contract) + dot(a[1], b[0], contract))


def wider(x):
    return jnp.concatenate([x, x], axis=-1)


def prepare_body(
    edge_hbm, feat_hbm, self_hbm, neigh_hbm, label_ref, low_ref, full_ref,
    edge_ref, feat_ref, self_ref, neigh_ref, sems,
):
    blocks, slots = edge_ref.shape[:2]
    tiles = [pltpu.make_async_copy(edge_hbm.at[b], edge_ref.at[b], sems.at[b]) for b in range(blocks)]
    dense = [
        pltpu.make_async_copy(source, target, sems.at[blocks + i])
        for i, (source, target) in enumerate(
            ((feat_hbm, feat_ref), (self_hbm, self_ref), (neigh_hbm, neigh_ref))
        )
    ]
    for c in tiles + dense:
        c.start()
    rows, width = feat_ref.shape
    classes = self_ref.shape[1]
    lines = label_ref.shape[0]
    columns = jnp.concatenate([label_ref[...].astype(F32), jnp.zeros((8 - lines % 8, 128), F32)], axis=0).T
    for r in range(lines):
        full_ref[r * 128 : (r + 1) * 128, classes + 128 :] = jnp.broadcast_to(columns[:, r : r + 1], (128, 128))
    for b in range(blocks):
        tiles[b].wait()
        wide = jnp.concatenate([edge_ref[b, s].astype(F32) for s in range(slots)], axis=1)
        low_ref[b * BLOCK : (b + 1) * BLOCK] = wide.astype(BF16)
        inverse = 1.0 / jnp.sum(wide, axis=1, keepdims=True)
        full_ref[b * BLOCK : (b + 1) * BLOCK, classes : classes + 128] = jnp.broadcast_to(inverse, (BLOCK, 128))
    for c in dense:
        c.wait()
    feat, own, neigh = feat_ref[...], self_ref[...], neigh_ref[...]
    full_ref[:, :classes] = dot3(halves(feat), halves(own))
    for k, x in enumerate(halves(feat.T)):
        low_ref[rows + k * width : rows + (k + 1) * width] = x
    for k, x in enumerate((neigh, neigh.T, own.T)):
        start = rows + (2 + k) * width
        low_ref[start : start + width] = jnp.concatenate(halves(x), axis=1)


def layer_body(*refs):
    pieces, (source_hbm, low_ref, full_ref), refs = refs[:12], refs[12:15], refs[15:]
    *made, direct_ref, mine_ref, passed_ref, table, mean, terms, source_ref, source_sem, piece_sems = refs
    sources = pltpu.make_async_copy(source_hbm, source_ref, source_sem)
    sources.start()
    per = pieces[0].shape[0]
    copies = [
        pltpu.make_async_copy(piece, table.at[pl.ds(i * per, per)], piece_sems.at[i])
        for i, piece in enumerate(pieces)
    ]
    for c in copies:
        c.start()
    rows, width = mean.shape
    classes = direct_ref.shape[1]
    blocks, slots = source_ref.shape
    me = lax.axis_index("rep")

    def named(b, s):
        return source_ref[b, s] ^ (me * blocks)

    terms[...] = jnp.zeros_like(terms)
    for c in [sources] + copies:
        c.wait()
    inverse = wider(full_ref[:, classes : classes + 128])
    for b in range(blocks):
        own = slice(b * BLOCK, (b + 1) * BLOCK)
        gathered = jnp.concatenate([table[named(b, s)] for s in range(slots)], axis=0)
        mean[own] = dot(low_ref[own], gathered) * inverse[own]

    def pair(k):
        x = low_ref[rows + (2 + k) * width : rows + (3 + k) * width]
        return x[:, :classes], x[:, classes:]

    neigh, neigh_t, own_t = [pair(k) for k in range(3)]
    mean_parts = halves(mean[...])
    logits = full_ref[:, :classes] + dot3(mean_parts, neigh)
    labels = lax.broadcasted_iota(jnp.int32, logits.shape, 1).astype(F32)
    target = jnp.where(labels == wider(full_ref[:, classes + 128 :]), 1.0, 0.0)
    residual = halves(1.0 / (1.0 + jnp.exp(-logits)) - target)
    spread = (dot3(residual, neigh_t) * inverse).astype(BF16)
    direct_ref[...] = dot3(residual, own_t)
    for b in range(blocks):
        own = slice(b * BLOCK, (b + 1) * BLOCK)
        contrib = dot(low_ref[own], spread[own], ROWS_BOTH)
        for s in range(slots):
            at = named(b, s)
            terms[at] = terms[at] + contrib[s * BLOCK : (s + 1) * BLOCK]

    for core in range(2):
        for place in range(6):
            rel = 2 + core if place < 3 else core
            region = (1, 2, 0)[place % 3]
            which, at = (2 * core, place) if place < 2 else (2 * core + 1, place - 2)
            made[which][at] = terms[pl.ds((region * 4 + rel) * per, per)].astype(BF16)

    self_part = dot3((low_ref[rows : rows + width], low_ref[rows + width : rows + 2 * width]), residual)
    neigh_part = dot3(mean_parts, residual, ROWS_BOTH)
    first = me % 2 == 0
    mine_ref[...] = jnp.where(first, self_part, neigh_part)
    passed_ref[...] = jnp.where(first, neigh_part, self_part)


def own_body(direct_ref, keep_ref, got_ref, half_ref, out_ref):
    both = keep_ref[3].astype(F32) + got_ref[3].astype(F32)
    out_ref[...] = direct_ref[...] + (both + half_ref[...].astype(F32))


def split_body(place_ref, *refs):
    outs = [r for r in refs if r.shape != refs[0].shape]
    total = tree_sum(r[...] for r in refs[: len(refs) - len(outs)])
    chunks = total.reshape(len(outs), *outs[0].shape)
    if len(outs) == 1:
        outs[0][...] = chunks[0]
        return
    for d, out in enumerate(outs):
        for c in range(len(outs)):

            @pl.when(place_ref[0] ^ d == c)
            def _():
                out[...] = chunks[c]


def add_body(a_ref, b_ref, sum_ref):
    sum_ref[...] = (a_ref[...].astype(F32) + b_ref[...].astype(F32)).astype(sum_ref.dtype)


def join_body(place_ref, *refs):
    out = refs[-1]
    rows = refs[0].shape[0]
    for d, chunk in enumerate(refs[:-1]):
        for c in range(len(refs) - 1):

            @pl.when(place_ref[0] ^ d == c)
            def _():
                out[c * rows : (c + 1) * rows] = chunk[...]


def tree_sum(values):
    values = list(values)
    while len(values) > 1:
        values = [sum(values[i + 1 : i + 2], values[i]) for i in range(0, len(values), 2)]
    return values[0]


def on_device(features, self_weight, neigh_weight, block_source, edge_weights, labels):
    rows, width = features.shape
    blocks, slots = block_source.shape
    classes = self_weight.shape[1]
    reps = lax.axis_size("rep")
    assert reps == 4
    me = lax.axis_index("rep").astype(jnp.int32)

    def swap(x, axis, d):
        return lax.ppermute(x, axis, [(i, i ^ d) for i in range(lax.axis_size(axis))])

    def core_swap(x):
        return swap(x, "rep", 1)

    def half_swap(x):
        return swap(x, "rep", 2)

    def up(x):
        cols = lax.axis_size("col")
        return lax.ppermute(x, "col", [(i, (i + 1) % cols) for i in range(cols)])

    def down(x):
        cols = lax.axis_size("col")
        return lax.ppermute(x, "col", [((i + 1) % cols, i) for i in range(cols)])

    own = features.astype(BF16).reshape(blocks, BLOCK, width)
    half, lower, upper, core = half_swap(own), up(own), down(own), core_swap(own)

    wide_cols = slots * BLOCK
    assert wide_cols == rows == 2 * width and classes == width
    low, full = call(
        prepare_body,
        (shape((2 * rows + 3 * width, wide_cols), BF16), shape((rows, classes + 256), F32)),
        (edge_weights, features, self_weight, neigh_weight, labels.reshape(rows // 128, 128)),
        [ANY] * 4 + [VMEM],
        [VMEM] * 2,
        scratch=[
            pltpu.VMEM(edge_weights.shape, jnp.int32),
            pltpu.VMEM(features.shape, F32),
            pltpu.VMEM(self_weight.shape, F32),
            pltpu.VMEM(neigh_weight.shape, F32),
            pltpu.SemaphoreType.DMA((blocks + 3,)),
        ],
        flops=6 * rows * width * classes,
        vmem=50,
    )
    half, lower, upper, core = (lax.optimization_barrier((x, full))[0] for x in (half, lower, upper, core))
    lower_half, upper_half = half_swap(lower), half_swap(upper)
    pieces = [
        own, core, half, core_swap(half),
        lower, core_swap(lower), lower_half, core_swap(lower_half),
        upper, core_swap(upper), upper_half, core_swap(upper_half),
    ]

    def piece_shape(*lead):
        return shape((*lead, blocks, BLOCK, width), BF16)

    weights = shape((width, classes), F32)
    keep_near, keep_rest, send_near, send_rest, direct, mine, passed = call(
        layer_body,
        (
            piece_shape(2), piece_shape(4), piece_shape(2), piece_shape(4),
            shape((rows, width), F32), weights, weights,
        ),
        (*pieces, block_source, low, full),
        [ANY] * 13 + [VMEM] * 2,
        [VMEM] * 7,
        scratch=[
            pltpu.VMEM((12 * blocks, BLOCK, width), BF16),
            pltpu.VMEM((rows, width), F32),
            pltpu.VMEM((12 * blocks, BLOCK, width), F32),
            pltpu.SMEM((blocks, slots), jnp.int32),
            pltpu.SemaphoreType.DMA(()),
            pltpu.SemaphoreType.DMA((12,)),
        ],
        flops=40 * rows * width * classes,
        vmem=24,
    )
    got_near, got_rest, got = core_swap(send_near), core_swap(send_rest), core_swap(passed)

    def both(a, b):
        return a.astype(F32) + b.astype(F32)

    lines, cols = lax.axis_size("row"), lax.axis_size("col")
    line = lax.axis_index("row").astype(jnp.int32).reshape(1)

    def split(parts):
        chunk = shape((parts[0].shape[0] // lines, classes), F32)
        return call(
            split_body,
            (chunk,) * lines,
            (line, *parts),
            [SMEM] + [VMEM] * len(parts),
            [VMEM] * lines,
            vmem=4,
        )

    def join(chunk):
        parts = [chunk] + [swap(chunk, "row", d) for d in range(1, lines)]
        (out,) = call(
            join_body,
            (shape((chunk.shape[0] * lines, classes), F32),),
            (line, *parts),
            [SMEM] + [VMEM] * lines,
            [VMEM],
            vmem=4,
        )
        return out

    def add(a, b, dtype=F32):
        (out,) = call(add_body, (shape(a.shape, dtype),), (a, b), [VMEM] * 2, [VMEM], vmem=4)
        return out

    def together(*values):
        return lax.optimization_barrier(values)

    near, got = together(both(keep_near, got_near).astype(BF16), got)
    half_near = half_swap(near)
    chunks = split((mine, got))
    part = chunks[0]
    for d in range(1, lines):
        part = add(part, swap(chunks[d].astype(BF16), "row", d), F32)
    step = 1
    while step < cols:
        part = add(part, swap(part, "col", step), BF16 if step == 1 else F32)
        step *= 2
    half_near, part, got_rest = together(half_near, part, got_rest)

    near = [both(keep_rest[1 + k], got_rest[1 + k]) + half_near[k].astype(F32) for k in range(2)]
    from_upper = down(near[0].astype(BF16))
    from_lower = up(near[1].astype(BF16))
    part = add(part, half_swap(part))
    whole = join(part)
    half_own = half_swap(both(keep_rest[0], got_rest[0]).astype(BF16))
    other = core_swap(whole)
    first = me % 2 == 0
    grad_self = jnp.where(first, whole, other)
    grad_neigh = jnp.where(first, other, whole)

    (own_terms,) = call(
        own_body,
        (shape((blocks, BLOCK, width), F32),),
        (direct.reshape(blocks, BLOCK, width), keep_rest, got_rest, half_own),
        [VMEM] * 4,
        [VMEM],
    )
    grad_features = own_terms + both(from_upper, from_lower)
    return grad_self, grad_neigh, grad_features.reshape(rows, width)


def solution(mesh):
    split = ("row", "col", "rep")
    return jax.shard_map(
        on_device,
        mesh=mesh,
        in_specs=(P(split, None), P(), P(), P(split, None), P(split, None, None, None), P(split)),
        out_specs=(P(), P(), P(split, None)),
        check_vma=False,
    )
```

```python
import functools

import jax
import jax.numpy as jnp
from jax import lax
from jax.experimental import pallas as pl
from jax.experimental.pallas import tpu as pltpu
from jax.sharding import PartitionSpec as P

BLOCK = 64
F32 = jnp.float32
BF16 = jnp.bfloat16
VMEM = pl.BlockSpec(memory_space=pltpu.VMEM)
SMEM = pl.BlockSpec(memory_space=pltpu.SMEM)
ANY = pl.BlockSpec(memory_space=pl.ANY)
ROWS_BOTH = ((0,), (0,))


def shape(dims, dtype):
    return jax.ShapeDtypeStruct(dims, dtype)


def call(body, out_shape, operands, in_specs, out_specs, scratch=(), flops=0, vmem=60):
    moved = sum(x.size * x.dtype.itemsize for x in list(operands) + list(out_shape)) if flops else 0
    return pl.pallas_call(
        body,
        out_shape=out_shape,
        in_specs=in_specs,
        out_specs=out_specs,
        scratch_shapes=scratch,
        compiler_params=pltpu.CompilerParams(vmem_limit_bytes=vmem << 20),
        cost_estimate=pl.CostEstimate(flops=flops, bytes_accessed=moved, transcendentals=0),
    )(*operands)


def dot(a, b, contract=((1,), (0,))):
    return lax.dot_general(a, b, (contract, ((), ())), preferred_element_type=F32)


def halves(x):
    high = x.astype(BF16)
    return high, (x - high.astype(F32)).astype(BF16)


def dot3(a, b, contract=((1,), (0,))):
    return dot(a[0], b[0], contract) + (dot(a[0], b[1], contract) + dot(a[1], b[0], contract))


def wider(x):
    return jnp.concatenate([x, x], axis=-1)


def prepare_body(
    edge_hbm, feat_hbm, self_hbm, neigh_hbm, label_ref, low_ref, full_ref,
    edge_ref, feat_ref, self_ref, neigh_ref, sems,
):
    blocks, slots = edge_ref.shape[:2]
    tiles = [pltpu.make_async_copy(edge_hbm.at[b], edge_ref.at[b], sems.at[b]) for b in range(blocks)]
    dense = [
        pltpu.make_async_copy(source, target, sems.at[blocks + i])
        for i, (source, target) in enumerate(
            ((feat_hbm, feat_ref), (self_hbm, self_ref), (neigh_hbm, neigh_ref))
        )
    ]
    for c in tiles + dense:
        c.start()
    rows, width = feat_ref.shape
    classes = self_ref.shape[1]
    lines = label_ref.shape[0]
    columns = jnp.concatenate([label_ref[...].astype(F32), jnp.zeros((8 - lines % 8, 128), F32)], axis=0).T
    for r in range(lines):
        full_ref[r * 128 : (r + 1) * 128, classes + 128 :] = jnp.broadcast_to(columns[:, r : r + 1], (128, 128))
    for b in range(blocks):
        tiles[b].wait()
        wide = jnp.concatenate([edge_ref[b, s].astype(F32) for s in range(slots)], axis=1)
        low_ref[b * BLOCK : (b + 1) * BLOCK] = wide.astype(BF16)
        inverse = 1.0 / jnp.sum(wide, axis=1, keepdims=True)
        full_ref[b * BLOCK : (b + 1) * BLOCK, classes : classes + 128] = jnp.broadcast_to(inverse, (BLOCK, 128))
    for c in dense:
        c.wait()
    feat, own, neigh = feat_ref[...], self_ref[...], neigh_ref[...]
    full_ref[:, :classes] = dot3(halves(feat), halves(own))
    for k, x in enumerate(halves(feat.T)):
        low_ref[rows + k * width : rows + (k + 1) * width] = x
    for k, x in enumerate((neigh, neigh.T, own.T)):
        start = rows + (2 + k) * width
        low_ref[start : start + width] = jnp.concatenate(halves(x), axis=1)


def layer_body(*refs):
    pieces, (source_hbm, low_ref, full_ref), refs = refs[:12], refs[12:15], refs[15:]
    *made, direct_ref, mine_ref, passed_ref, table, mean, terms, source_ref, source_sem, piece_sems = refs
    sources = pltpu.make_async_copy(source_hbm, source_ref, source_sem)
    sources.start()
    per = pieces[0].shape[0]
    copies = [
        pltpu.make_async_copy(piece, table.at[pl.ds(i * per, per)], piece_sems.at[i])
        for i, piece in enumerate(pieces)
    ]
    for c in copies:
        c.start()
    rows, width = mean.shape
    classes = direct_ref.shape[1]
    blocks, slots = source_ref.shape
    me = lax.axis_index("rep")

    def named(b, s):
        return source_ref[b, s] ^ (me * blocks)

    terms[...] = jnp.zeros_like(terms)
    for c in [sources] + copies:
        c.wait()
    inverse = wider(full_ref[:, classes : classes + 128])
    for b in range(blocks):
        own = slice(b * BLOCK, (b + 1) * BLOCK)
        gathered = jnp.concatenate([table[named(b, s)] for s in range(slots)], axis=0)
        mean[own] = dot(low_ref[own], gathered) * inverse[own]

    def pair(k):
        x = low_ref[rows + (2 + k) * width : rows + (3 + k) * width]
        return x[:, :classes], x[:, classes:]

    neigh, neigh_t, own_t = [pair(k) for k in range(3)]
    mean_parts = halves(mean[...])
    logits = full_ref[:, :classes] + dot3(mean_parts, neigh)
    labels = lax.broadcasted_iota(jnp.int32, logits.shape, 1).astype(F32)
    target = jnp.where(labels == wider(full_ref[:, classes + 128 :]), 1.0, 0.0)
    residual = halves(1.0 / (1.0 + jnp.exp(-logits)) - target)
    spread = (dot3(residual, neigh_t) * inverse).astype(BF16)
    direct_ref[...] = dot3(residual, own_t)
    for b in range(blocks):
        own = slice(b * BLOCK, (b + 1) * BLOCK)
        contrib = dot(low_ref[own], spread[own], ROWS_BOTH)
        for s in range(slots):
            at = named(b, s)
            terms[at] = terms[at] + contrib[s * BLOCK : (s + 1) * BLOCK]

    for core in range(2):
        for place in range(6):
            rel = 2 + core if place < 3 else core
            region = (1, 2, 0)[place % 3]
            which, at = (2 * core, place) if place < 2 else (2 * core + 1, place - 2)
            made[which][at] = terms[pl.ds((region * 4 + rel) * per, per)].astype(BF16)

    self_part = dot3((low_ref[rows : rows + width], low_ref[rows + width : rows + 2 * width]), residual)
    neigh_part = dot3(mean_parts, residual, ROWS_BOTH)
    first = me % 2 == 0
    mine_ref[...] = jnp.where(first, self_part, neigh_part)
    passed_ref[...] = jnp.where(first, neigh_part, self_part)


def split_body(place_ref, *refs):
    outs = [r for r in refs if r.shape != refs[0].shape]
    total = tree_sum(r[...] for r in refs[: len(refs) - len(outs)])
    chunks = total.reshape(len(outs), *outs[0].shape)
    if len(outs) == 1:
        outs[0][...] = chunks[0]
        return
    for d, out in enumerate(outs):
        for c in range(len(outs)):

            @pl.when(place_ref[0] ^ d == c)
            def _():
                out[...] = chunks[c]


def add_body(a_ref, b_ref, sum_ref):
    sum_ref[...] = (a_ref[...].astype(F32) + b_ref[...].astype(F32)).astype(sum_ref.dtype)


def join_body(place_ref, *refs):
    out = refs[-1]
    rows = refs[0].shape[0]
    for d, chunk in enumerate(refs[:-1]):
        for c in range(len(refs) - 1):

            @pl.when(place_ref[0] ^ d == c)
            def _():
                out[c * rows : (c + 1) * rows] = chunk[...]


def tree_sum(values):
    values = list(values)
    while len(values) > 1:
        values = [sum(values[i + 1 : i + 2], values[i]) for i in range(0, len(values), 2)]
    return values[0]


def on_device(features, self_weight, neigh_weight, block_source, edge_weights, labels):
    rows, width = features.shape
    blocks, slots = block_source.shape
    classes = self_weight.shape[1]
    reps = lax.axis_size("rep")
    assert reps == 4
    me = lax.axis_index("rep").astype(jnp.int32)

    def swap(x, axis, d):
        return lax.ppermute(x, axis, [(i, i ^ d) for i in range(lax.axis_size(axis))])

    def core_swap(x):
        return swap(x, "rep", 1)

    def half_swap(x):
        return swap(x, "rep", 2)

    def up(x):
        cols = lax.axis_size("col")
        return lax.ppermute(x, "col", [(i, (i + 1) % cols) for i in range(cols)])

    def down(x):
        cols = lax.axis_size("col")
        return lax.ppermute(x, "col", [((i + 1) % cols, i) for i in range(cols)])

    own = features.astype(BF16).reshape(blocks, BLOCK, width)
    half, lower, upper, core = half_swap(own), up(own), down(own), core_swap(own)

    wide_cols = slots * BLOCK
    assert wide_cols == rows == 2 * width and classes == width
    low, full = call(
        prepare_body,
        (shape((2 * rows + 3 * width, wide_cols), BF16), shape((rows, classes + 256), F32)),
        (edge_weights, features, self_weight, neigh_weight, labels.reshape(rows // 128, 128)),
        [ANY] * 4 + [VMEM],
        [VMEM] * 2,
        scratch=[
            pltpu.VMEM(edge_weights.shape, jnp.int32),
            pltpu.VMEM(features.shape, F32),
            pltpu.VMEM(self_weight.shape, F32),
            pltpu.VMEM(neigh_weight.shape, F32),
            pltpu.SemaphoreType.DMA((blocks + 3,)),
        ],
        flops=6 * rows * width * classes,
        vmem=50,
    )
    half, lower, upper, core = (lax.optimization_barrier((x, full))[0] for x in (half, lower, upper, core))
    lower_half, upper_half = half_swap(lower), half_swap(upper)
    pieces = [
        own, core, half, core_swap(half),
        lower, core_swap(lower), lower_half, core_swap(lower_half),
        upper, core_swap(upper), upper_half, core_swap(upper_half),
    ]

    def piece_shape(*lead):
        return shape((*lead, blocks, BLOCK, width), BF16)

    weights = shape((width, classes), F32)
    keep_near, keep_rest, send_near, send_rest, direct, mine, passed = call(
        layer_body,
        (
            piece_shape(2), piece_shape(4), piece_shape(2), piece_shape(4),
            shape((rows, width), F32), weights, weights,
        ),
        (*pieces, block_source, low, full),
        [ANY] * 13 + [VMEM] * 2,
        [VMEM] * 7,
        scratch=[
            pltpu.VMEM((12 * blocks, BLOCK, width), BF16),
            pltpu.VMEM((rows, width), F32),
            pltpu.VMEM((12 * blocks, BLOCK, width), F32),
            pltpu.SMEM((blocks, slots), jnp.int32),
            pltpu.SemaphoreType.DMA(()),
            pltpu.SemaphoreType.DMA((12,)),
        ],
        flops=40 * rows * width * classes,
        vmem=24,
    )
    got_near, got_rest, got = core_swap(send_near), core_swap(send_rest), core_swap(passed)

    def both(a, b):
        return a.astype(F32) + b.astype(F32)

    lines, cols = lax.axis_size("row"), lax.axis_size("col")
    line = lax.axis_index("row").astype(jnp.int32).reshape(1)

    def split(parts):
        chunk = shape((parts[0].shape[0] // lines, classes), F32)
        return call(
            split_body,
            (chunk,) * lines,
            (line, *parts),
            [SMEM] + [VMEM] * len(parts),
            [VMEM] * lines,
            vmem=4,
        )

    def join(chunk):
        parts = [chunk] + [swap(chunk, "row", d) for d in range(1, lines)]
        (out,) = call(
            join_body,
            (shape((chunk.shape[0] * lines, classes), F32),),
            (line, *parts),
            [SMEM] + [VMEM] * lines,
            [VMEM],
            vmem=4,
        )
        return out

    def add(a, b, dtype=F32):
        (out,) = call(add_body, (shape(a.shape, dtype),), (a, b), [VMEM] * 2, [VMEM], vmem=4)
        return out

    def together(*values):
        return lax.optimization_barrier(values)

    near, got = together(both(keep_near, got_near).astype(BF16), got)
    half_near = half_swap(near)
    chunks = split((mine, got))
    part = chunks[0]
    for d in range(1, lines):
        part = add(part, swap(chunks[d].astype(BF16), "row", d), F32)
    step = 1
    while step < cols:
        part = add(part, swap(part, "col", step), BF16 if step == 1 else F32)
        step *= 2
    half_near, part, got_rest = together(half_near, part, got_rest)

    near = [both(keep_rest[1 + k], got_rest[1 + k]) + half_near[k].astype(F32) for k in range(2)]
    from_upper = down(near[0].astype(BF16))
    from_lower = up(near[1].astype(BF16))
    part = add(part, half_swap(part))
    whole = join(part)
    half_own = half_swap(both(keep_rest[0], got_rest[0]).astype(BF16))
    other = core_swap(whole)
    first = me % 2 == 0
    grad_self = jnp.where(first, whole, other)
    grad_neigh = jnp.where(first, other, whole)

    own_terms = direct.reshape(blocks, BLOCK, width) + both(keep_rest[3], got_rest[3]) + half_own.astype(F32)
    own_terms, from_upper = together(own_terms, from_upper)
    grad_features = own_terms + both(from_upper, from_lower)
    return grad_self, grad_neigh, grad_features.reshape(rows, width)


def solution(mesh):
    split = ("row", "col", "rep")
    return jax.shard_map(
        on_device,
        mesh=mesh,
        in_specs=(P(split, None), P(), P(), P(split, None), P(split, None, None, None), P(split)),
        out_specs=(P(), P(), P(split, None)),
        check_vma=False,
    )
```

```python
import functools

import jax
import jax.numpy as jnp
from jax import lax
from jax.experimental import pallas as pl
from jax.experimental.pallas import tpu as pltpu
from jax.sharding import PartitionSpec as P

BLOCK = 64
F32 = jnp.float32
BF16 = jnp.bfloat16
VMEM = pl.BlockSpec(memory_space=pltpu.VMEM)
SMEM = pl.BlockSpec(memory_space=pltpu.SMEM)
ANY = pl.BlockSpec(memory_space=pl.ANY)
ROWS_BOTH = ((0,), (0,))


def shape(dims, dtype):
    return jax.ShapeDtypeStruct(dims, dtype)


def call(body, out_shape, operands, in_specs, out_specs, scratch=(), flops=0, vmem=60):
    moved = sum(x.size * x.dtype.itemsize for x in list(operands) + list(out_shape)) if flops else 0
    return pl.pallas_call(
        body,
        out_shape=out_shape,
        in_specs=in_specs,
        out_specs=out_specs,
        scratch_shapes=scratch,
        compiler_params=pltpu.CompilerParams(vmem_limit_bytes=vmem << 20),
        cost_estimate=pl.CostEstimate(flops=flops, bytes_accessed=moved, transcendentals=0),
    )(*operands)


def dot(a, b, contract=((1,), (0,))):
    return lax.dot_general(a, b, (contract, ((), ())), preferred_element_type=F32)


def halves(x):
    high = x.astype(BF16)
    return high, (x - high.astype(F32)).astype(BF16)


def dot3(a, b, contract=((1,), (0,))):
    return dot(a[0], b[0], contract) + (dot(a[0], b[1], contract) + dot(a[1], b[0], contract))


def wider(x):
    return jnp.concatenate([x, x], axis=-1)


def prepare_body(
    edge_hbm, feat_hbm, self_hbm, neigh_hbm, label_ref, low_ref, full_ref,
    edge_ref, feat_ref, self_ref, neigh_ref, sems,
):
    blocks, slots = edge_ref.shape[:2]
    tiles = [pltpu.make_async_copy(edge_hbm.at[b], edge_ref.at[b], sems.at[b]) for b in range(blocks)]
    dense = [
        pltpu.make_async_copy(source, target, sems.at[blocks + i])
        for i, (source, target) in enumerate(
            ((feat_hbm, feat_ref), (self_hbm, self_ref), (neigh_hbm, neigh_ref))
        )
    ]
    for c in tiles + dense:
        c.start()
    rows, width = feat_ref.shape
    classes = self_ref.shape[1]
    lines = label_ref.shape[0]
    columns = jnp.concatenate([label_ref[...].astype(F32), jnp.zeros((8 - lines % 8, 128), F32)], axis=0).T
    for r in range(lines):
        full_ref[r * 128 : (r + 1) * 128, classes + 128 :] = jnp.broadcast_to(columns[:, r : r + 1], (128, 128))
    for b in range(blocks):
        tiles[b].wait()
        wide = jnp.concatenate([edge_ref[b, s].astype(F32) for s in range(slots)], axis=1)
        low_ref[b * BLOCK : (b + 1) * BLOCK] = wide.astype(BF16)
        inverse = 1.0 / jnp.sum(wide, axis=1, keepdims=True)
        full_ref[b * BLOCK : (b + 1) * BLOCK, classes : classes + 128] = jnp.broadcast_to(inverse, (BLOCK, 128))
    for c in dense:
        c.wait()
    feat, own, neigh = feat_ref[...], self_ref[...], neigh_ref[...]
    full_ref[:, :classes] = dot3(halves(feat), halves(own))
    for k, x in enumerate(halves(feat.T)):
        low_ref[rows + k * width : rows + (k + 1) * width] = x
    for k, x in enumerate((neigh, neigh.T, own.T)):
        start = rows + (2 + k) * width
        low_ref[start : start + width] = jnp.concatenate(halves(x), axis=1)


def layer_body(*refs):
    pieces, (source_hbm, low_ref, full_ref), refs = refs[:12], refs[12:15], refs[15:]
    *made, direct_ref, mine_ref, passed_ref, table, mean, terms, source_ref, source_sem, piece_sems = refs
    sources = pltpu.make_async_copy(source_hbm, source_ref, source_sem)
    sources.start()
    per = pieces[0].shape[0]
    copies = [
        pltpu.make_async_copy(piece, table.at[pl.ds(i * per, per)], piece_sems.at[i])
        for i, piece in enumerate(pieces)
    ]
    for c in copies:
        c.start()
    rows, width = mean.shape
    classes = direct_ref.shape[1]
    blocks, slots = source_ref.shape
    me = lax.axis_index("rep")

    def named(b, s):
        return source_ref[b, s] ^ (me * blocks)

    terms[...] = jnp.zeros_like(terms)
    for c in [sources] + copies:
        c.wait()
    inverse = wider(full_ref[:, classes : classes + 128])
    for b in range(blocks):
        own = slice(b * BLOCK, (b + 1) * BLOCK)
        gathered = jnp.concatenate([table[named(b, s)] for s in range(slots)], axis=0)
        mean[own] = dot(low_ref[own], gathered) * inverse[own]

    def pair(k):
        x = low_ref[rows + (2 + k) * width : rows + (3 + k) * width]
        return x[:, :classes], x[:, classes:]

    neigh, neigh_t, own_t = [pair(k) for k in range(3)]
    mean_parts = halves(mean[...])
    logits = full_ref[:, :classes] + dot3(mean_parts, neigh)
    labels = lax.broadcasted_iota(jnp.int32, logits.shape, 1).astype(F32)
    target = jnp.where(labels == wider(full_ref[:, classes + 128 :]), 1.0, 0.0)
    residual = halves(1.0 / (1.0 + jnp.exp(-logits)) - target)
    spread = (dot3(residual, neigh_t) * inverse).astype(BF16)
    direct_ref[...] = dot3(residual, own_t)
    for b in range(blocks):
        own = slice(b * BLOCK, (b + 1) * BLOCK)
        contrib = dot(low_ref[own], spread[own], ROWS_BOTH)
        for s in range(slots):
            at = named(b, s)
            terms[at] = terms[at] + contrib[s * BLOCK : (s + 1) * BLOCK]

    for core in range(2):
        for place in range(6):
            rel = 2 + core if place < 3 else core
            region = (1, 2, 0)[place % 3]
            which, at = (2 * core, place) if place < 2 else (2 * core + 1, place - 2)
            made[which][at] = terms[pl.ds((region * 4 + rel) * per, per)].astype(BF16)

    self_part = dot3((low_ref[rows : rows + width], low_ref[rows + width : rows + 2 * width]), residual)
    neigh_part = dot3(mean_parts, residual, ROWS_BOTH)
    first = me % 2 == 0
    mine_ref[...] = jnp.where(first, self_part, neigh_part)
    passed_ref[...] = jnp.where(first, neigh_part, self_part)


def split_body(place_ref, *refs):
    outs = [r for r in refs if r.shape != refs[0].shape]
    total = tree_sum(r[...] for r in refs[: len(refs) - len(outs)])
    chunks = total.reshape(len(outs), *outs[0].shape)
    if len(outs) == 1:
        outs[0][...] = chunks[0]
        return
    for d, out in enumerate(outs):
        for c in range(len(outs)):

            @pl.when(place_ref[0] ^ d == c)
            def _():
                out[...] = chunks[c]


def add_body(a_ref, b_ref, sum_ref):
    sum_ref[...] = (a_ref[...].astype(F32) + b_ref[...].astype(F32)).astype(sum_ref.dtype)


def join_body(place_ref, *refs):
    out = refs[-1]
    rows = refs[0].shape[0]
    for d, chunk in enumerate(refs[:-1]):
        for c in range(len(refs) - 1):

            @pl.when(place_ref[0] ^ d == c)
            def _():
                out[c * rows : (c + 1) * rows] = chunk[...]


def tree_sum(values):
    values = list(values)
    while len(values) > 1:
        values = [sum(values[i + 1 : i + 2], values[i]) for i in range(0, len(values), 2)]
    return values[0]


def on_device(features, self_weight, neigh_weight, block_source, edge_weights, labels):
    rows, width = features.shape
    blocks, slots = block_source.shape
    classes = self_weight.shape[1]
    reps = lax.axis_size("rep")
    assert reps == 4
    me = lax.axis_index("rep").astype(jnp.int32)

    def swap(x, axis, d):
        return lax.ppermute(x, axis, [(i, i ^ d) for i in range(lax.axis_size(axis))])

    def core_swap(x):
        return swap(x, "rep", 1)

    def half_swap(x):
        return swap(x, "rep", 2)

    def up(x):
        cols = lax.axis_size("col")
        return lax.ppermute(x, "col", [(i, (i + 1) % cols) for i in range(cols)])

    def down(x):
        cols = lax.axis_size("col")
        return lax.ppermute(x, "col", [((i + 1) % cols, i) for i in range(cols)])

    own = features.astype(BF16).reshape(blocks, BLOCK, width)
    half, lower, upper, core = half_swap(own), up(own), down(own), core_swap(own)

    wide_cols = slots * BLOCK
    assert wide_cols == rows == 2 * width and classes == width
    low, full = call(
        prepare_body,
        (shape((2 * rows + 3 * width, wide_cols), BF16), shape((rows, classes + 256), F32)),
        (edge_weights, features, self_weight, neigh_weight, labels.reshape(rows // 128, 128)),
        [ANY] * 4 + [VMEM],
        [VMEM] * 2,
        scratch=[
            pltpu.VMEM(edge_weights.shape, jnp.int32),
            pltpu.VMEM(features.shape, F32),
            pltpu.VMEM(self_weight.shape, F32),
            pltpu.VMEM(neigh_weight.shape, F32),
            pltpu.SemaphoreType.DMA((blocks + 3,)),
        ],
        flops=6 * rows * width * classes,
        vmem=50,
    )
    half, lower, core = (lax.optimization_barrier((x, full))[0] for x in (half, lower, core))
    lower_half, upper_half = half_swap(lower), half_swap(upper)
    pieces = [
        own, core, half, core_swap(half),
        lower, core_swap(lower), lower_half, core_swap(lower_half),
        upper, core_swap(upper), upper_half, core_swap(upper_half),
    ]

    def piece_shape(*lead):
        return shape((*lead, blocks, BLOCK, width), BF16)

    weights = shape((width, classes), F32)
    keep_near, keep_rest, send_near, send_rest, direct, mine, passed = call(
        layer_body,
        (
            piece_shape(2), piece_shape(4), piece_shape(2), piece_shape(4),
            shape((rows, width), F32), weights, weights,
        ),
        (*pieces, block_source, low, full),
        [ANY] * 13 + [VMEM] * 2,
        [VMEM] * 7,
        scratch=[
            pltpu.VMEM((12 * blocks, BLOCK, width), BF16),
            pltpu.VMEM((rows, width), F32),
            pltpu.VMEM((12 * blocks, BLOCK, width), F32),
            pltpu.SMEM((blocks, slots), jnp.int32),
            pltpu.SemaphoreType.DMA(()),
            pltpu.SemaphoreType.DMA((12,)),
        ],
        flops=40 * rows * width * classes,
        vmem=24,
    )
    got_near, got_rest, got = core_swap(send_near), core_swap(send_rest), core_swap(passed)

    def both(a, b):
        return a.astype(F32) + b.astype(F32)

    lines, cols = lax.axis_size("row"), lax.axis_size("col")
    line = lax.axis_index("row").astype(jnp.int32).reshape(1)

    def split(parts):
        chunk = shape((parts[0].shape[0] // lines, classes), F32)
        return call(
            split_body,
            (chunk,) * lines,
            (line, *parts),
            [SMEM] + [VMEM] * len(parts),
            [VMEM] * lines,
            vmem=4,
        )

    def join(chunk):
        parts = [chunk] + [swap(chunk, "row", d) for d in range(1, lines)]
        (out,) = call(
            join_body,
            (shape((chunk.shape[0] * lines, classes), F32),),
            (line, *parts),
            [SMEM] + [VMEM] * lines,
            [VMEM],
            vmem=4,
        )
        return out

    def add(a, b, dtype=F32):
        (out,) = call(add_body, (shape(a.shape, dtype),), (a, b), [VMEM] * 2, [VMEM], vmem=4)
        return out

    def together(*values):
        return lax.optimization_barrier(values)

    near, got = together(both(keep_near, got_near).astype(BF16), got)
    half_near = half_swap(near)
    chunks = split((mine, got))
    part = chunks[0]
    for d in range(1, lines):
        part = add(part, swap(chunks[d].astype(BF16), "row", d), F32)
    step = 1
    while step < cols:
        part = add(part, swap(part, "col", step), BF16 if step == 1 else F32)
        step *= 2
    half_near, part, got_rest = together(half_near, part, got_rest)

    near = [both(keep_rest[1 + k], got_rest[1 + k]) + half_near[k].astype(F32) for k in range(2)]
    from_upper = down(near[0].astype(BF16))
    from_lower = up(near[1].astype(BF16))
    part = add(part, half_swap(part))
    whole = join(part)
    half_own = half_swap(both(keep_rest[0], got_rest[0]).astype(BF16))
    other = core_swap(whole)
    first = me % 2 == 0
    grad_self = jnp.where(first, whole, other)
    grad_neigh = jnp.where(first, other, whole)

    own_terms = direct.reshape(blocks, BLOCK, width) + both(keep_rest[3], got_rest[3]) + half_own.astype(F32)
    own_terms, from_upper = together(own_terms, from_upper)
    grad_features = own_terms + both(from_upper, from_lower)
    return grad_self, grad_neigh, grad_features.reshape(rows, width)


def solution(mesh):
    split = ("row", "col", "rep")
    return jax.shard_map(
        on_device,
        mesh=mesh,
        in_specs=(P(split, None), P(), P(), P(split, None), P(split, None, None, None), P(split)),
        out_specs=(P(), P(), P(split, None)),
        check_vma=False,
    )
```
